32 devices in a mesh: grp: 2 (over x), tile: 8 (over z, y), pos: 2 (over core).
Axes of the slice: x: 2, y: 2, z: 4, core: 2. Of those that a mesh axis runs over, the one named last changes fastest.
Arguments:
- object_slices: bfloat16 [2, 4, 2048, 512], P('pos', 'grp', 'tile'), parts along dimension 1, may hold values from -6 to 6
- probe: bfloat16 [4, 256, 256], P('grp'), parts along dimension 0, may hold values from -4 to 4
- intensity: bfloat16 [8, 16, 2, 256, 256], P('tile', 'grp', 'pos'), parts along dimension 1, may hold values from 0.099609375 to 2
- scan_rows: int32 [8, 16, 2], P('tile', 'grp', 'pos'), parts along dimension 1, may hold values from 0 to 255, as said below
- scan_cols: int32 [8, 16, 2], P('tile', 'grp', 'pos'), parts along dimension 1, may hold values from 0 to 256
- counts: int32 [2, 8], P('grp', 'tile'), parts along dimension 0, may hold values from 1 to 16, as said below
Outputs:
- object_grad: float32 [2, 4, 2048, 512], P('pos', 'grp', 'tile'), parts along dimension 1
- probe_grad: float32 [4, 256, 256], P('grp'), parts along dimension 0
The draws below stay inside these ranges and needn't reach their ends.
There are 2 independent parts, one for each index of `grp`. The reference program is written for one: setup_inputs(seed, part) draws one part's arguments, and reference() takes and returns one part's arrays. A program takes and returns all parts, laid end to end along the dimension named above; each array names one. Nothing has to cross between parts.
Inputs may be any that keep to these rules, and one draw needn't show every extreme that they name: `scan_rows`: offsets of the last strip's positions are at most 0, so every window lies inside the object. `counts`: slots whose position is not live hold arbitrary values, which must be ignored; some strip is full and some strip has one live position.
All inputs are finite; a program needn't handle non-finite values.
Results may differ from the reference program's by a relative error of at most 0.0098.
Values may be sent and summed in bfloat16 or wider, within the bound.
No kernel may reach another device: no remote copies, remote signals or barrier semaphores. Data moves between devices by JAX's collectives and lax.ppermute only.
A program may use at most 64 MiB of HBM per device.

```python
import math
import jax
import jax.numpy as jnp
from jax import lax

PROBE = 256
BAND = 32
SLICES = 2
STRIP = 256
NY = 512
SLOTS = 8
TILES = 8
CORES = 2
GROUP = 16
NX = 2048


def draw_scan_rows(key, part):
    rows = jax.random.randint(key, (TILES, SLOTS, CORES), 0, STRIP, dtype=jnp.int32)
    last = jax.random.randint(jax.random.fold_in(key, 11), (SLOTS, CORES), 0, STRIP - PROBE + 1, dtype=jnp.int32)
    rows = rows.at[TILES - 1].set(last)
    rows = rows.at[0, 0, 0].set(STRIP - 1)
    rows = rows.at[1, 0, 0].set(0)
    return rows


def draw_scan_cols(key, part):
    cols = jax.random.randint(key, (TILES, SLOTS, CORES), 0, NY - PROBE + 1, dtype=jnp.int32)
    cols = cols.at[0, 0, 0].set(NY - PROBE)
    cols = cols.at[1, 0, 0].set(0)
    return cols


def draw_counts(key, part):
    shifts = jax.random.randint(key, (TILES,), 0, 4, dtype=jnp.int32)
    counts = jnp.maximum(jnp.right_shift(jnp.full((TILES,), GROUP, jnp.int32), shifts), 1)
    full_tile = jax.random.randint(jax.random.fold_in(key, 21), (), 0, TILES, dtype=jnp.int32)
    step_away = jax.random.randint(jax.random.fold_in(key, 22), (), 0, TILES - 1, dtype=jnp.int32)
    lone_tile = (full_tile + 1 + step_away) % TILES
    counts = counts.at[full_tile].set(GROUP)
    counts = counts.at[lone_tile].set(1)
    return counts.reshape(1, TILES)


def block_scale(key, shape, pieces, smallest, largest):
    def one(axis_at, parts):
        draws = jax.random.uniform(jax.random.fold_in(jax.random.fold_in(key, 6), axis_at), (parts,), jnp.float32, smallest / len(pieces), largest / len(pieces))
        return jnp.repeat(jnp.exp(draws), shape[axis_at] // parts).reshape((-1,) + (1,) * (len(shape) - axis_at - 1))

    loudness = one(*pieces[0])
    for cut in pieces[1:]:
        loudness = loudness * one(*cut)
    return loudness


def centred(key, dims, width, bound, cuts=(), kind=jnp.bfloat16):
    loudness = block_scale(key, dims, cuts, -0.22, 0.18) if cuts else 1.0
    result = jax.random.normal(key, dims, jnp.float32) * width * loudness
    return jnp.minimum(jnp.maximum(result, -bound), bound).astype(kind)


def setup_inputs(seed: int = 0, part: int = 0) -> dict:
    key_of = jax.random.split(jax.random.key(seed), 7)
    part_keys = jax.random.split(jax.random.fold_in(key_of[6], part), 7)
    object_slices = centred(part_keys[0], (SLICES, 2, NX, NY), 0.8, 6.0, ((0, 2), (2, 8)))
    probe = centred(part_keys[1], (2, PROBE, PROBE), 0.5, 4.0)
    intensity = jnp.clip(jnp.exp(math.log(2.0) - 2.9996462 * jax.random.uniform(part_keys[2], (TILES, SLOTS, CORES, PROBE, PROBE), jnp.float32) ** block_scale(part_keys[2], (TILES, SLOTS, CORES, PROBE, PROBE), ((0, 8), (2, 2)), -0.2, 0.2)), 0.099609375, 2.0).astype(jnp.bfloat16)
    scan_rows = draw_scan_rows(jax.random.fold_in(jax.random.fold_in(key_of[6], part), 71), part)
    scan_cols = draw_scan_cols(jax.random.fold_in(jax.random.fold_in(key_of[6], part), 71), part)
    counts = draw_counts(jax.random.fold_in(jax.random.fold_in(key_of[6], part), 71), part)
    return {"object_slices": object_slices, "probe": probe, "intensity": intensity, "scan_rows": scan_rows, "scan_cols": scan_cols, "counts": counts}


def make_tables(size, band):
    index = jnp.arange(size, dtype=jnp.int32)
    offset = index[:, None] - index[None, :]
    inside = (jnp.abs(offset) <= band).astype(jnp.float32)
    offset_f = offset.astype(jnp.float32)
    phase = math.pi * offset_f * offset_f / (2.0 * band)
    scale = 1.0 / math.sqrt(2 * band + 1)
    prop_re = (jnp.cos(phase) * inside * scale).astype(jnp.bfloat16)
    prop_im = (jnp.sin(phase) * inside * scale).astype(jnp.bfloat16)
    product = index[:, None] * index[None, :] % size
    angle = -2.0 * math.pi * product.astype(jnp.float32) / size
    four_re = (jnp.cos(angle) / math.sqrt(size)).astype(jnp.bfloat16)
    four_im = (jnp.sin(angle) / math.sqrt(size)).astype(jnp.bfloat16)
    return (prop_re, prop_im, -prop_im, four_re, four_im, -four_im)

def matdot(left, right):
    return jnp.dot(left, right, preferred_element_type=jnp.float32)

def left_mul(mat_re, mat_im, val_re, val_im):
    return (matdot(mat_re, val_re) - matdot(mat_im, val_im), matdot(mat_re, val_im) + matdot(mat_im, val_re))

def right_mul(val_re, val_im, mat_re, mat_im):
    return (matdot(val_re, mat_re) - matdot(val_im, mat_im), matdot(val_re, mat_im) + matdot(val_im, mat_re))

def to_half(value):
    return value.astype(jnp.bfloat16)

def position_terms(window, probe, measured, table_set):
    prop_re, prop_im, prop_neg, four_re, four_im, four_neg = table_set
    first_re = window[0, 0].astype(jnp.float32)
    first_im = window[0, 1].astype(jnp.float32)
    second_re = window[1, 0].astype(jnp.float32)
    second_im = window[1, 1].astype(jnp.float32)
    probe_re = probe[0].astype(jnp.float32)
    probe_im = probe[1].astype(jnp.float32)
    enter_re = to_half(probe_re * first_re - probe_im * first_im)
    enter_im = to_half(probe_re * first_im + probe_im * first_re)
    half_re, half_im = left_mul(prop_re, prop_im, enter_re, enter_im)
    after_re, after_im = right_mul(to_half(half_re), to_half(half_im), prop_re, prop_im)
    exit_re = to_half(after_re * second_re - after_im * second_im)
    exit_im = to_half(after_re * second_im + after_im * second_re)
    far_re, far_im = left_mul(four_re, four_im, exit_re, exit_im)
    wave_re, wave_im = right_mul(to_half(far_re), to_half(far_im), four_re, four_im)
    misfit = wave_re * wave_re + wave_im * wave_im - measured.astype(jnp.float32)
    back_re = to_half(misfit * wave_re)
    back_im = to_half(misfit * wave_im)
    near_re, near_im = left_mul(four_re, four_neg, back_re, back_im)
    exit_gre, exit_gim = right_mul(to_half(near_re), to_half(near_im), four_re, four_neg)
    grad_second = jnp.stack([exit_gre * after_re + exit_gim * after_im, exit_gim * after_re - exit_gre * after_im])
    mid_re = to_half(exit_gre * second_re + exit_gim * second_im)
    mid_im = to_half(exit_gim * second_re - exit_gre * second_im)
    prev_re, prev_im = left_mul(prop_re, prop_neg, mid_re, mid_im)
    enter_gre, enter_gim = right_mul(to_half(prev_re), to_half(prev_im), prop_re, prop_neg)
    grad_first = jnp.stack([enter_gre * probe_re + enter_gim * probe_im, enter_gim * probe_re - enter_gre * probe_im])
    probe_term = jnp.stack([enter_gre * first_re + enter_gim * first_im, enter_gim * first_re - enter_gre * first_im])
    return (jnp.stack([grad_first, grad_second]), probe_term)

def reference(object_slices, probe, intensity, scan_rows, scan_cols, counts):
    table_set = make_tables(PROBE, BAND)
    total = TILES * SLOTS * CORES
    flat_index = jnp.arange(total, dtype=jnp.int32)
    tile_of = flat_index // (SLOTS * CORES)
    slot_of = flat_index // CORES % SLOTS
    core_of = flat_index % CORES
    live = slot_of * CORES + core_of < counts[0][tile_of]
    rows_all = (tile_of * STRIP + scan_rows.reshape(-1)).astype(jnp.int32)
    cols_all = scan_cols.reshape(-1).astype(jnp.int32)
    measured_all = intensity.reshape(total, PROBE, PROBE)
    zero = jnp.zeros((), jnp.int32)

    def visit(carry, item):

        def work(state):
            grad_obj, grad_probe = state
            row_at = rows_all[item]
            col_at = cols_all[item]
            starts = (zero, zero, row_at, col_at)
            window = lax.dynamic_slice(object_slices, starts, (SLICES, 2, PROBE, PROBE))
            grad_win, probe_term = position_terms(window, probe, measured_all[item], table_set)
            previous = lax.dynamic_slice(grad_obj, starts, (SLICES, 2, PROBE, PROBE))
            grad_obj = lax.dynamic_update_slice(grad_obj, previous + grad_win, starts)
            return (grad_obj, grad_probe + probe_term)
        return (lax.cond(live[item], work, lambda state: state, carry), None)
    start = (jnp.zeros((SLICES, 2, NX, NY), jnp.float32), jnp.zeros((2, PROBE, PROBE), jnp.float32))
    (grad_obj, grad_probe), _ = lax.scan(visit, start, flat_index)
    return (grad_obj, grad_probe / math.sqrt(TILES * SLOTS * CORES))
```

```python
import math

import jax
import jax.numpy as jnp
import ml_dtypes
import numpy as np
from jax import lax
from jax.experimental import pallas as pl
from jax.experimental.pallas import tpu as pltpu
from jax.sharding import PartitionSpec as P

BAND = 32
LANES = 128
CHUNK = 16
WIN_CHUNK = 32
VMEM_BYTES = 56 * 1024 * 1024
f32 = jnp.float32
bf16 = jnp.bfloat16


def tables(size):
    index = np.arange(size, dtype=np.int32)
    offset = index[:, None] - index[None, :]
    inside = (np.abs(offset) <= BAND).astype(np.float32)
    offset_f = offset.astype(np.float32)
    phase = (np.float32(math.pi) * offset_f * offset_f / np.float32(2.0 * BAND)).astype(np.float32)
    scale = np.float32(1.0 / math.sqrt(2 * BAND + 1))
    prop_re = np.cos(phase) * inside * scale
    prop_im = np.sin(phase) * inside * scale
    product = (index[:, None] * index[None, :]) % size
    angle = (np.float32(-2.0 * math.pi) * product.astype(np.float32) / np.float32(size)).astype(np.float32)
    root = np.float32(math.sqrt(size))
    return prop_re, prop_im, np.cos(angle) / root, np.sin(angle) / root


def packed(mat_re, mat_im):
    n, k = mat_re.shape
    upper = np.concatenate([mat_re, -mat_im], axis=1).reshape(n // CHUNK, 1, CHUNK, 2 * k)
    lower = np.concatenate([mat_im, mat_re], axis=1).reshape(n // CHUNK, 1, CHUNK, 2 * k)
    both = np.concatenate([upper, lower], axis=1).reshape(2 * n, 2 * k)
    return both.astype(np.float32).astype(ml_dtypes.bfloat16)


def constants(size):
    half = size // 2
    kr, ki, fr, fi = tables(size)
    near, far = half + BAND, half - BAND
    prop = [
        packed(kr[:near, :half], ki[:near, :half]),
        packed(kr[far:, half:], ki[far:, half:]),
        packed(kr[:near, :half], -ki[:near, :half]),
        packed(kr[far:, half:], -ki[far:, half:]),
    ]
    four = [
        packed(fr[0::2, :half], fi[0::2, :half]),
        packed(fr[1::2, :half], fi[1::2, :half]),
        packed(fr[:half, 0::2], -fi[:half, 0::2]),
        packed(fr[:half, 1::2], -fi[:half, 1::2]),
    ]
    order = np.concatenate([np.arange(0, size, 2), np.arange(1, size, 2)])
    perm = np.eye(size, dtype=np.float32)[order].astype(ml_dtypes.bfloat16)
    return np.stack(prop), np.stack(four), perm


def nt(left, right):
    return lax.dot_general(left, right, (((1,), (1,)), ((), ())), preferred_element_type=f32)


def kernel(
    rows_ref, cols_ref, info_ref,
    own_ref, other_ref, halo_own_ref, halo_other_ref, probe_ref, meas_ref, prop_ref, four_ref, perm_ref,
    strip_ref, tail_ref, send_ref, probe_out_ref,
    ext, acc, win, wave, x_a, x_b, pro,
):
    size = probe_ref.shape[1]
    half = size // 2
    strip = own_ref.shape[1]
    ny = own_ref.shape[2]
    blocks = ny // LANES
    steps = size // CHUNK
    core = info_ref[0]
    live = info_ref[1]

    for at, source in ((0, own_ref), (1, other_ref)):
        which = core if at == 0 else 1 - core
        lower = halo_own_ref if at == 0 else halo_other_ref
        for part in range(2):
            for block in range(blocks):
                lanes = slice(block * LANES, (block + 1) * LANES)
                ext[which, part, block, :strip, :] = source[part, :, lanes].astype(f32)
                ext[which, part, block, strip:, :] = lower[part, :, lanes].astype(f32)
    acc[...] = jnp.zeros(acc.shape, f32)
    probe_out_ref[...] = jnp.zeros(probe_out_ref.shape, f32)
    pro[...] = probe_ref[...].astype(f32)

    def banded(base, source):
        first = nt(prop_ref[base], source[:, :size])
        second = nt(prop_ref[base + 1], source[:, size:])
        skip = (half - BAND) // CHUNK
        stop = (half + BAND) // CHUNK

        def at(j):
            out = []
            for part in range(2):
                value = None
                if j < stop:
                    lo = (2 * j + part) * CHUNK
                    value = first[lo : lo + CHUNK]
                if j >= skip:
                    lo = (2 * (j - skip) + part) * CHUNK
                    more = second[lo : lo + CHUNK]
                    value = more if value is None else value + more
                out.append(value)
            return out

        return at

    def halves(base, source):
        first = nt(four_ref[base], source[:, :size])
        second = nt(four_ref[base + 1], source[:, size:])

        def at(j):
            lo = 2 * j * CHUNK
            return (
                (first[lo : lo + CHUNK], first[lo + CHUNK : lo + 2 * CHUNK]),
                (second[lo : lo + CHUNK], second[lo + CHUNK : lo + 2 * CHUNK]),
            )

        return at

    def put(target, lo, re, im):
        target[lo : lo + CHUNK, :] = jnp.concatenate(
            [re[:, :half], im[:, :half], re[:, half:], im[:, half:]], axis=1
        ).astype(bf16)

    def put_butterfly(target, lo, re, im):
        target[lo : lo + CHUNK, :] = jnp.concatenate(
            [
                re[:, :half] + re[:, half:],
                im[:, :half] + im[:, half:],
                re[:, :half] - re[:, half:],
                im[:, :half] - im[:, half:],
            ],
            axis=1,
        ).astype(bf16)

    def visit(slot, _):
        row = rows_ref[slot]
        col = cols_ref[slot]
        block_at = lax.shift_right_logical(col, 7)
        shift = jnp.bitwise_and(col, LANES - 1)
        back = jnp.bitwise_and(LANES - shift, LANES - 1)
        keep = lax.broadcasted_iota(jnp.int32, (WIN_CHUNK, LANES), 1) < LANES - shift
        low = lax.broadcasted_iota(jnp.int32, (CHUNK, LANES), 1) < shift

        def scatter(which, lo, parts):
            for part, value in enumerate(parts):
                left = pltpu.roll(value[:, :LANES], shift, 1)
                right = pltpu.roll(value[:, LANES:], shift, 1)
                pieces = (
                    jnp.where(low, 0.0, left),
                    jnp.where(low, left, right),
                    jnp.where(low, right, 0.0),
                )
                for i, piece in enumerate(pieces):
                    at = (which, part, block_at + i, pl.ds(row + lo, CHUNK), slice(None))
                    acc[at] = acc[at] + piece

        for lo in range(0, size, WIN_CHUNK):
            span = slice(lo, lo + WIN_CHUNK)
            for which in range(2):
                for part in range(2):
                    loaded = [
                        pltpu.roll(ext[which, part, block_at + i, pl.ds(row + lo, WIN_CHUNK), :], back, 1)
                        for i in range(3)
                    ]
                    win[which, part, span, :LANES] = jnp.where(keep, loaded[0], loaded[1])
                    win[which, part, span, LANES:] = jnp.where(keep, loaded[1], loaded[2])

        for j in range(steps):
            span = slice(j * CHUNK, (j + 1) * CHUNK)
            pr, pi = pro[0, span], pro[1, span]
            wr, wi = win[0, 0, span], win[0, 1, span]
            put(x_a, j * CHUNK, pr * wr - pi * wi, pr * wi + pi * wr)

        at = banded(0, x_a[...])
        for j in range(steps):
            re, im = at(j)
            put(x_b, j * CHUNK, re, im)

        at = banded(0, x_b[...])
        for j in range(steps):
            span = slice(j * CHUNK, (j + 1) * CHUNK)
            re, im = at(j)
            wave[0, span] = re
            wave[1, span] = im
            wr, wi = win[1, 0, span], win[1, 1, span]
            put_butterfly(x_a, j * CHUNK, re * wr - im * wi, re * wi + im * wr)

        at = halves(0, x_a[...])
        for j in range(steps // 2):
            even, odd = at(j)
            put_butterfly(x_b, j * CHUNK, *even)
            put_butterfly(x_b, half + j * CHUNK, *odd)

        at = halves(0, x_b[...])
        for j in range(steps // 2):
            for side, (re, im) in enumerate(at(j)):
                lo = side * half + j * CHUNK
                misfit = re * re + im * im - meas_ref[slot, lo : lo + CHUNK, :].astype(f32)
                put(x_a, lo, misfit * re, misfit * im)

        at = halves(2, x_a[...])
        for j in range(steps // 2):
            (er, ei), (dr, di) = at(j)
            put(x_b, j * CHUNK, er + dr, ei + di)
            put(x_b, half + j * CHUNK, er - dr, ei - di)

        at = halves(2, x_b[...])
        for j in range(steps // 2):
            (er, ei), (dr, di) = at(j)
            for side in range(2):
                lo = side * half + j * CHUNK
                span = slice(lo, lo + CHUNK)
                re, im = (er + dr, ei + di) if side == 0 else (er - dr, ei - di)
                br, bi = wave[0, span], wave[1, span]
                wr, wi = win[1, 0, span], win[1, 1, span]
                scatter(1, lo, (re * br + im * bi, im * br - re * bi))
                put(x_a, lo, re * wr + im * wi, im * wr - re * wi)

        at = banded(2, x_a[...])
        for j in range(steps):
            re, im = at(j)
            put(x_b, j * CHUNK, re, im)

        at = banded(2, x_b[...])
        for j in range(steps):
            lo = j * CHUNK
            span = slice(lo, lo + CHUNK)
            re, im = at(j)
            pr, pi = pro[0, span], pro[1, span]
            wr, wi = win[0, 0, span], win[0, 1, span]
            scatter(0, lo, (re * pr + im * pi, im * pr - re * pi))
            probe_out_ref[0, span] = probe_out_ref[0, span] + (re * wr + im * wi)
            probe_out_ref[1, span] = probe_out_ref[1, span] + (im * wr - re * wi)
        return 0

    lax.fori_loop(0, live, visit, 0)

    for part in range(2):
        for block in range(blocks):
            lanes = slice(block * LANES, (block + 1) * LANES)
            strip_ref[part, :, lanes] = acc[core, part, block, :strip, :]
            tail_ref[part, :, lanes] = acc[core, part, block, strip:, :]
            send_ref[part, :, lanes] = acc[1 - core, part, block, :, :].astype(bf16)


def swap(value):
    return lax.ppermute(value, "pos", [(0, 1), (1, 0)])


def shift_tile(value, by):
    peers = lax.axis_size("tile")
    return lax.ppermute(value, "tile", [(i, i + by) for i in range(peers) if 0 <= i + by < peers])


def local(object_slices, probe, intensity, scan_rows, scan_cols, counts):
    strip, ny = object_slices.shape[2:]
    size = probe.shape[1]
    slots = intensity.shape[1]
    cores = lax.axis_size("pos")
    core = lax.axis_index("pos")
    prop, four, perm = constants(size)
    own = object_slices[0]
    other = swap(own)
    halo_own = shift_tile(own, -1)
    halo_other = swap(halo_own)
    order = np.concatenate([np.arange(0, size, 2), np.arange(1, size, 2)])
    measured = intensity.reshape(slots, size // 2, 2, size // 2, 2).transpose(0, 2, 1, 4, 3).reshape(slots, size, size)
    live = jnp.minimum(jnp.maximum(counts[0, 0] - core + cores - 1, 0) // cores, slots)
    info = jnp.stack([core, live]).astype(jnp.int32)
    vmem = pl.BlockSpec(memory_space=pltpu.VMEM)
    smem = pl.BlockSpec(memory_space=pltpu.SMEM)
    blocks = ny // LANES + 1
    strip_grad, tail, send, grad_probe = pl.pallas_call(
        kernel,
        out_shape=(
            jax.ShapeDtypeStruct((2, strip, ny), f32),
            jax.ShapeDtypeStruct((2, strip, ny), f32),
            jax.ShapeDtypeStruct((2, 2 * strip, ny), bf16),
            jax.ShapeDtypeStruct((2, size, size), f32),
        ),
        in_specs=[smem] * 3 + [vmem] * 9,
        out_specs=(vmem,) * 4,
        scratch_shapes=[
            pltpu.VMEM((2, 2, blocks, 2 * strip, LANES), f32),
            pltpu.VMEM((2, 2, blocks, 2 * strip, LANES), f32),
            pltpu.VMEM((2, 2, size, size), f32),
            pltpu.VMEM((2, size, size), f32),
            pltpu.VMEM((size, 2 * size), bf16),
            pltpu.VMEM((size, 2 * size), bf16),
            pltpu.VMEM((2, size, size), f32),
        ],
        compiler_params=pltpu.CompilerParams(vmem_limit_bytes=VMEM_BYTES),
    )(
        scan_rows[0, :, 0], scan_cols[0, :, 0], info,
        own, other, halo_own, halo_other, probe, measured,
        jnp.asarray(prop), jnp.asarray(four), jnp.asarray(perm),
    )
    got = swap(send).astype(f32)
    tail_sum = (tail + got[:, strip:]).astype(bf16)
    from_above = shift_tile(tail_sum, 1).astype(f32)
    owned = (strip_grad + got[:, :strip] + from_above)[None]
    total_slots = lax.axis_size("tile") * slots * cores

    mine = lax.dynamic_index_in_dim(grad_probe, core, 0, keepdims=False)
    theirs = lax.dynamic_index_in_dim(grad_probe, 1 - core, 0, keepdims=False)
    part = mine + swap(theirs)
    peers = lax.axis_size("tile")
    step = 1
    while step < peers:
        part = part + lax.ppermute(part, "tile", [(i, i ^ step) for i in range(peers)])
        step *= 2
    part = part / math.sqrt(total_slots)
    again = swap(part)
    probe_total = jnp.where(core == 0, jnp.stack([part, again]), jnp.stack([again, part]))
    return owned, probe_total


def solution(mesh):
    placed = (
        P("pos", "grp", "tile", None),
        P("grp", None, None),
        P("tile", "grp", "pos", None, None),
        P("tile", "grp", "pos"),
        P("tile", "grp", "pos"),
        P("grp", "tile"),
    )
    return jax.shard_map(
        local,
        mesh=mesh,
        in_specs=placed,
        out_specs=(P("pos", "grp", "tile", None), P("grp", None, None)),
        check_vma=False,
    )
```

```python
import math

import jax
import jax.numpy as jnp
import ml_dtypes
import numpy as np
from jax import lax
from jax.experimental import pallas as pl
from jax.experimental.pallas import tpu as pltpu
from jax.sharding import PartitionSpec as P

BAND = 32
LANES = 128
CHUNK = 16
WIN_CHUNK = 32
GROUP = 4
VMEM_BYTES = 40 * 1024 * 1024
f32 = jnp.float32
bf16 = jnp.bfloat16


def tables(size):
    index = np.arange(size, dtype=np.int32)
    offset = index[:, None] - index[None, :]
    inside = (np.abs(offset) <= BAND).astype(np.float32)
    offset_f = offset.astype(np.float32)
    phase = (np.float32(math.pi) * offset_f * offset_f / np.float32(2.0 * BAND)).astype(np.float32)
    scale = np.float32(1.0 / math.sqrt(2 * BAND + 1))
    prop_re = np.cos(phase) * inside * scale
    prop_im = np.sin(phase) * inside * scale
    product = (index[:, None] * index[None, :]) % size
    angle = (np.float32(-2.0 * math.pi) * product.astype(np.float32) / np.float32(size)).astype(np.float32)
    root = np.float32(math.sqrt(size))
    return prop_re, prop_im, np.cos(angle) / root, np.sin(angle) / root


def packed(mat_re, mat_im):
    n, k = mat_re.shape
    upper = np.concatenate([mat_re, -mat_im], axis=1).reshape(n // CHUNK, 1, CHUNK, 2 * k)
    lower = np.concatenate([mat_im, mat_re], axis=1).reshape(n // CHUNK, 1, CHUNK, 2 * k)
    both = np.concatenate([upper, lower], axis=1).reshape(2 * n, 2 * k)
    return both.astype(np.float32).astype(ml_dtypes.bfloat16)


def constants(size):
    half = size // 2
    kr, ki, fr, fi = tables(size)
    near, far = half + BAND, half - BAND
    prop = [
        packed(kr[:near, :half], ki[:near, :half]),
        packed(kr[far:, half:], ki[far:, half:]),
        packed(kr[:near, :half], -ki[:near, :half]),
        packed(kr[far:, half:], -ki[far:, half:]),
    ]
    four = [
        packed(fr[0::2, :half], fi[0::2, :half]),
        packed(fr[1::2, :half], fi[1::2, :half]),
        packed(fr[:half, 0::2], -fi[:half, 0::2]),
        packed(fr[:half, 1::2], -fi[:half, 1::2]),
    ]
    order = np.concatenate([np.arange(0, size, 2), np.arange(1, size, 2)])
    perm = np.eye(size, dtype=np.float32)[order].astype(ml_dtypes.bfloat16)
    return np.stack(prop), np.stack(four), perm


def nt(left, right):
    return lax.dot_general(left, right, (((1,), (1,)), ((), ())), preferred_element_type=f32)


def banded(prop_ref, base, source):
    size = source.shape[1] // 2
    skip = (size // 2 - BAND) // CHUNK
    stop = (size // 2 + BAND) // CHUNK
    first = nt(prop_ref[base], source[:, :size])
    second = nt(prop_ref[base + 1], source[:, size:])

    def at(j):
        out = []
        for part in range(2):
            value = None
            if j < stop:
                lo = (2 * j + part) * CHUNK
                value = first[lo : lo + CHUNK]
            if j >= skip:
                lo = (2 * (j - skip) + part) * CHUNK
                more = second[lo : lo + CHUNK]
                value = more if value is None else value + more
            out.append(value)
        return out

    return at


def halves(four_ref, base, source):
    size = source.shape[1] // 2
    first = nt(four_ref[base], source[:, :size])
    second = nt(four_ref[base + 1], source[:, size:])

    def at(j):
        lo = 2 * j * CHUNK
        return (
            (first[lo : lo + CHUNK], first[lo + CHUNK : lo + 2 * CHUNK]),
            (second[lo : lo + CHUNK], second[lo + CHUNK : lo + 2 * CHUNK]),
        )

    return at


def put(target, lo, re, im):
    half = re.shape[1] // 2
    target[lo : lo + CHUNK, :] = jnp.concatenate(
        [re[:, :half], im[:, :half], re[:, half:], im[:, half:]], axis=1
    ).astype(bf16)


def put_butterfly(target, lo, re, im):
    half = re.shape[1] // 2
    target[lo : lo + CHUNK, :] = jnp.concatenate(
        [
            re[:, :half] + re[:, half:],
            im[:, :half] + im[:, half:],
            re[:, :half] - re[:, half:],
            im[:, :half] - im[:, half:],
        ],
        axis=1,
    ).astype(bf16)


class Place:
    def __init__(self, row, col):
        self.row = row
        self.block = lax.shift_right_logical(col, 7)
        self.shift = jnp.bitwise_and(col, LANES - 1)


def fill(ext, core, strips, halos):
    strip = strips[0].shape[1]
    for side in range(2):

        @pl.when(core == side)
        def _():
            for part in range(2):
                for block in range(strips[side].shape[2] // LANES):
                    lanes = slice(block * LANES, (block + 1) * LANES)
                    ext[part, block, :strip, :] = strips[side][part, :, lanes].astype(f32)
                    ext[part, block, strip:, :] = halos[side][part, :, lanes].astype(f32)


def window(ext, win, place):
    size = win.shape[1]
    back = jnp.bitwise_and(LANES - place.shift, LANES - 1)
    keep = lax.broadcasted_iota(jnp.int32, (WIN_CHUNK, LANES), 1) < LANES - place.shift
    for lo in range(0, size, WIN_CHUNK):
        span = slice(lo, lo + WIN_CHUNK)
        for part in range(2):
            loaded = [
                pltpu.roll(ext[part, place.block + i, pl.ds(place.row + lo, WIN_CHUNK), :], back, 1)
                for i in range(3)
            ]
            win[part, span, :LANES] = jnp.where(keep, loaded[0], loaded[1])
            win[part, span, LANES:] = jnp.where(keep, loaded[1], loaded[2])


def scatter(acc, place, lo, parts):
    low = lax.broadcasted_iota(jnp.int32, (CHUNK, LANES), 1) < place.shift
    for part, value in enumerate(parts):
        left = pltpu.roll(value[:, :LANES], place.shift, 1)
        right = pltpu.roll(value[:, LANES:], place.shift, 1)
        pieces = (jnp.where(low, 0.0, left), jnp.where(low, left, right), jnp.where(low, right, 0.0))
        for i, piece in enumerate(pieces):
            at = (part, place.block + i, pl.ds(place.row + lo, CHUNK), slice(None))
            acc[at] = acc[at] + piece


def emit(acc, strip_ref, tail_ref, send_strip_ref, send_tail_ref):
    strip, ny = strip_ref.shape[1:]
    for part in range(2):
        for block in range(ny // LANES):
            lanes = slice(block * LANES, (block + 1) * LANES)
            upper = acc[part, block, :strip, :]
            lower = acc[part, block, strip:, :]
            strip_ref[part, :, lanes] = upper
            tail_ref[part, :, lanes] = lower
            send_strip_ref[part, :, lanes] = upper.astype(bf16)
            send_tail_ref[part, :, lanes] = lower.astype(bf16)


def members(step, live, slots):
    for g in range(GROUP):
        slot = step * GROUP + g
        yield jnp.minimum(slot, live - 1), jnp.where(slot < live, slot, slots + g - 1), slot < live


def prepare_kernel(meas_ref, perm_ref, own_ref, out_ref, own_out_ref):
    own_out_ref[...] = own_ref[...]
    perm = perm_ref[...]
    for slot in range(meas_ref.shape[0]):
        rows = jnp.dot(perm, meas_ref[slot], preferred_element_type=f32).astype(bf16)
        out_ref[slot] = nt(rows, perm).astype(bf16)


def forward_kernel(
    rows_ref, cols_ref, info_ref,
    own_ref, other_ref, halo_ref, passed_ref, probe_ref, prop_ref,
    wave_ref,
    ext, win, x_a, x_b, pro,
):
    size = probe_ref.shape[1]
    steps = size // CHUNK
    core, live = info_ref[0], info_ref[1]
    slots = wave_ref.shape[0]
    fill(ext, core, (own_ref, other_ref), (halo_ref, passed_ref))
    pro[...] = probe_ref[...].astype(f32)

    def visit(step, _):
        group = list(members(step, live, slots))
        for g, (slot, _, _) in enumerate(group):
            window(ext, win.at[g], Place(rows_ref[slot], cols_ref[slot]))
            for j in range(steps):
                span = slice(j * CHUNK, (j + 1) * CHUNK)
                pr, pi = pro[0, span], pro[1, span]
                wr, wi = win[g, 0, span], win[g, 1, span]
                put(x_a.at[g], j * CHUNK, pr * wr - pi * wi, pr * wi + pi * wr)
        for g in range(GROUP):
            at = banded(prop_ref, 0, x_a[g])
            for j in range(steps):
                put(x_b.at[g], j * CHUNK, *at(j))
        for g, (slot, _, _) in enumerate(group):
            at = banded(prop_ref, 0, x_b[g])
            for j in range(steps):
                re, im = at(j)
                span = slice(j * CHUNK, (j + 1) * CHUNK)
                wave_ref[slot, 0, span] = re.astype(bf16)
                wave_ref[slot, 1, span] = im.astype(bf16)
        return 0

    lax.fori_loop(0, (live + GROUP - 1) // GROUP, visit, 0)


def detector_kernel(
    rows_ref, cols_ref, info_ref,
    own_ref, other_ref, halo_ref, passed_ref, wave_ref, meas_ref, prop_ref, four_ref,
    back_ref, strip_ref, tail_ref, send_strip_ref, send_tail_ref,
    ext, acc, win, x_a, x_b,
):
    size = meas_ref.shape[1]
    half = size // 2
    steps = size // CHUNK
    core, live = info_ref[0], info_ref[1]
    slots = wave_ref.shape[0]
    fill(ext, core, (other_ref, own_ref), (passed_ref, halo_ref))
    acc[...] = jnp.zeros(acc.shape, f32)

    def visit(step, _):
        group = list(members(step, live, slots))
        places = [Place(rows_ref[slot], cols_ref[slot]) for slot, _, _ in group]
        for g, (slot, _, _) in enumerate(group):
            window(ext, win.at[g], places[g])
            for j in range(steps):
                span = slice(j * CHUNK, (j + 1) * CHUNK)
                br, bi = wave_ref[slot, 0, span].astype(f32), wave_ref[slot, 1, span].astype(f32)
                wr, wi = win[g, 0, span], win[g, 1, span]
                put_butterfly(x_a.at[g], j * CHUNK, br * wr - bi * wi, br * wi + bi * wr)
        for g in range(GROUP):
            at = halves(four_ref, 0, x_a[g])
            for j in range(steps // 2):
                even, odd = at(j)
                put_butterfly(x_b.at[g], j * CHUNK, *even)
                put_butterfly(x_b.at[g], half + j * CHUNK, *odd)
        for g, (slot, _, valid) in enumerate(group):
            at = halves(four_ref, 0, x_b[g])
            factor = jnp.where(valid, 1.0, 0.0).astype(f32)
            for j in range(steps // 2):
                for side, (re, im) in enumerate(at(j)):
                    lo = side * half + j * CHUNK
                    misfit = re * re + im * im - meas_ref[slot, lo : lo + CHUNK, :].astype(f32)
                    misfit = misfit * factor
                    put(x_a.at[g], lo, misfit * re, misfit * im)
        for g in range(GROUP):
            at = halves(four_ref, 2, x_a[g])
            for j in range(steps // 2):
                (er, ei), (dr, di) = at(j)
                put(x_b.at[g], j * CHUNK, er + dr, ei + di)
                put(x_b.at[g], half + j * CHUNK, er - dr, ei - di)
        for g, (slot, target, _) in enumerate(group):
            at = halves(four_ref, 2, x_b[g])
            for j in range(steps // 2):
                (er, ei), (dr, di) = at(j)
                for side in range(2):
                    lo = side * half + j * CHUNK
                    span = slice(lo, lo + CHUNK)
                    re, im = (er + dr, ei + di) if side == 0 else (er - dr, ei - di)
                    br, bi = wave_ref[slot, 0, span].astype(f32), wave_ref[slot, 1, span].astype(f32)
                    wr, wi = win[g, 0, span], win[g, 1, span]
                    put(back_ref.at[target], lo, re * wr + im * wi, im * wr - re * wi)
                    scatter(acc, places[g], lo, (re * br + im * bi, im * br - re * bi))
        return 0

    lax.fori_loop(0, (live + GROUP - 1) // GROUP, visit, 0)
    emit(acc, strip_ref, tail_ref, send_strip_ref, send_tail_ref)


def backward_kernel(
    rows_ref, cols_ref, info_ref,
    own_ref, other_ref, halo_ref, passed_ref, back_ref, probe_ref, prop_ref,
    strip_ref, tail_ref, send_strip_ref, send_tail_ref, mine_ref, theirs_ref,
    ext, acc, win, x_b, pro, pacc,
):
    size = probe_ref.shape[1]
    steps = size // CHUNK
    core, live = info_ref[0], info_ref[1]
    slots = back_ref.shape[0] - GROUP + 1
    fill(ext, core, (own_ref, other_ref), (halo_ref, passed_ref))
    acc[...] = jnp.zeros(acc.shape, f32)
    pacc[...] = jnp.zeros(pacc.shape, f32)
    pro[...] = probe_ref[...].astype(f32)

    def visit(step, _):
        group = list(members(step, live, slots))
        places = [Place(rows_ref[slot], cols_ref[slot]) for slot, _, _ in group]
        for g, (slot, source, _) in enumerate(group):
            window(ext, win.at[g], places[g])
            at = banded(prop_ref, 2, back_ref[source])
            for j in range(steps):
                put(x_b.at[g], j * CHUNK, *at(j))
        for g in range(GROUP):
            at = banded(prop_ref, 2, x_b[g])
            for j in range(steps):
                lo = j * CHUNK
                span = slice(lo, lo + CHUNK)
                re, im = at(j)
                pr, pi = pro[0, span], pro[1, span]
                wr, wi = win[g, 0, span], win[g, 1, span]
                scatter(acc, places[g], lo, (re * pr + im * pi, im * pr - re * pi))
                pacc[0, span] = pacc[0, span] + (re * wr + im * wi)
                pacc[1, span] = pacc[1, span] + (im * wr - re * wi)
        return 0

    lax.fori_loop(0, (live + GROUP - 1) // GROUP, visit, 0)
    emit(acc, strip_ref, tail_ref, send_strip_ref, send_tail_ref)
    mine_ref[...] = pacc[core]
    theirs_ref[...] = pacc[1 - core].astype(bf16)


def swap(value):
    return lax.ppermute(value, "pos", [(0, 1), (1, 0)])


def across(value, start):
    return lax.ppermute(value, "pos", [(start, 1 - start)])


def shift_tile(value, core, by):
    peers, cores = lax.axis_size("tile"), lax.axis_size("pos")
    pairs = [(i * cores + core, (i + by) * cores + core) for i in range(peers) if 0 <= i + by < peers]
    return lax.ppermute(value, ("tile", "pos"), pairs)


def sum_over_tiles(value):
    peers = lax.axis_size("tile")
    step = 1
    while step < peers:
        half = value.astype(bf16)
        got = lax.ppermute(half, "tile", [(i, i ^ step) for i in range(peers)])
        value = half.astype(f32) + got.astype(f32)
        step *= 2
    return value


def call(body, results, operands, scalars, scratch, flops):
    vmem = pl.BlockSpec(memory_space=pltpu.VMEM)
    smem = pl.BlockSpec(memory_space=pltpu.SMEM)
    moved = sum(math.prod(x.shape) * x.dtype.itemsize for x in list(operands) + list(results))
    return pl.pallas_call(
        body,
        out_shape=tuple(results),
        in_specs=[smem] * len(scalars) + [vmem] * len(operands),
        out_specs=(vmem,) * len(results),
        scratch_shapes=scratch,
        cost_estimate=pl.CostEstimate(flops=flops, bytes_accessed=moved, transcendentals=0),
        compiler_params=pltpu.CompilerParams(vmem_limit_bytes=VMEM_BYTES),
    )(*scalars, *operands)


def local(object_slices, probe, intensity, scan_rows, scan_cols, counts):
    strip, ny = object_slices.shape[2:]
    size = probe.shape[1]
    slots = intensity.shape[1]
    cores = lax.axis_size("pos")
    core = lax.axis_index("pos")
    prop, four, perm = (jnp.asarray(t) for t in constants(size))
    sds = jax.ShapeDtypeStruct
    own = object_slices[0]
    live = jnp.minimum(jnp.maximum(counts[0, 0] - core + cores - 1, 0) // cores, slots)
    info = jnp.stack([core, live]).astype(jnp.int32)
    scalars = (scan_rows[0, :, 0], scan_cols[0, :, 0], info)
    blocks = ny // LANES + 1
    cube = 2 * size**3

    halo0 = shift_tile(own, 0, -1)
    other = swap(own)
    passed0 = across(halo0, 0)
    measured, own_later = call(
        prepare_kernel,
        (sds((slots, size, size), bf16), sds(own.shape, bf16)),
        (intensity.reshape(slots, size, size), perm, own),
        (), [], 2 * slots * cube,
    )
    halo1 = shift_tile(own_later, 1, -1)
    passed1 = across(halo1, 1)

    ext = pltpu.VMEM((2, blocks, 2 * strip, LANES), f32)
    win = pltpu.VMEM((GROUP, 2, size, size), f32)
    half_wave = pltpu.VMEM((GROUP, size, 2 * size), bf16)
    full = pltpu.VMEM((2, size, size), f32)
    slice_outs = (
        sds((2, strip, ny), f32), sds((2, strip, ny), f32), sds((2, strip, ny), bf16), sds((2, strip, ny), bf16),
    )
    (wave,) = call(
        forward_kernel,
        (sds((slots, 2, size, size), bf16),),
        (own, other, halo0, passed0, probe, prop),
        scalars, [ext, win, half_wave, half_wave, full], 5 * slots * cube,
    )
    back, strip1, tail1, send_strip1, send_tail1 = call(
        detector_kernel,
        (sds((slots + GROUP - 1, size, 2 * size), bf16),) + slice_outs,
        (own, other, halo1, passed1, wave, measured, prop, four),
        scalars, [ext, ext, win, half_wave, half_wave], 8 * slots * cube,
    )
    got_tail1 = across(send_tail1, 0).astype(f32)
    above1 = shift_tile((tail1 + got_tail1).astype(bf16), 1, 1)
    got_strip1 = across(send_strip1, 0)
    strip0, tail0, send_strip0, send_tail0, mine, theirs = call(
        backward_kernel,
        slice_outs + (sds((size, size), f32), sds((size, size), bf16)),
        (own, other, halo0, passed0, back, probe, prop),
        scalars, [ext, ext, win, half_wave, full, full], 5 * slots * cube,
    )
    part = mine + swap(theirs).astype(f32)
    got_tail0 = across(send_tail0, 1).astype(f32)
    above0 = shift_tile((tail0 + got_tail0).astype(bf16), 0, 1)
    got_strip0 = across(send_strip0, 1)
    owned = jnp.where(core == 0, strip0, strip1)
    for more in (got_strip0, got_strip1, above0, above1):
        owned = owned + more.astype(f32)

    total_slots = lax.axis_size("tile") * slots * cores
    part = sum_over_tiles(part) / math.sqrt(total_slots)
    again = swap(part)
    probe_total = jnp.where(core == 0, jnp.stack([part, again]), jnp.stack([again, part]))
    return owned[None], probe_total


def solution(mesh):
    placed = (
        P("pos", "grp", "tile", None),
        P("grp", None, None),
        P("tile", "grp", "pos", None, None),
        P("tile", "grp", "pos"),
        P("tile", "grp", "pos"),
        P("grp", "tile"),
    )
    return jax.shard_map(
        local,
        mesh=mesh,
        in_specs=placed,
        out_specs=(P("pos", "grp", "tile", None), P("grp", None, None)),
        check_vma=False,
    )
```

```python
import functools
import math

import jax
import jax.numpy as jnp
import ml_dtypes
import numpy as np
from jax import lax
from jax.experimental import pallas as pl
from jax.experimental.pallas import tpu as pltpu
from jax.sharding import PartitionSpec as P

BAND = 32
LANES = 128
CHUNK = 16
WIN_CHUNK = 32
GROUP = 4
MIB = 1024 * 1024
f32 = jnp.float32
bf16 = jnp.bfloat16


def tables(size):
    index = np.arange(size, dtype=np.int32)
    offset = index[:, None] - index[None, :]
    inside = (np.abs(offset) <= BAND).astype(np.float32)
    offset_f = offset.astype(np.float32)
    phase = (np.float32(math.pi) * offset_f * offset_f / np.float32(2.0 * BAND)).astype(np.float32)
    scale = np.float32(1.0 / math.sqrt(2 * BAND + 1))
    prop_re = np.cos(phase) * inside * scale
    prop_im = np.sin(phase) * inside * scale
    product = (index[:, None] * index[None, :]) % size
    angle = (np.float32(-2.0 * math.pi) * product.astype(np.float32) / np.float32(size)).astype(np.float32)
    root = np.float32(math.sqrt(size))
    return prop_re, prop_im, np.cos(angle) / root, np.sin(angle) / root


def packed(mat_re, mat_im):
    n, k = mat_re.shape
    upper = np.concatenate([mat_re, -mat_im], axis=1).reshape(n // CHUNK, 1, CHUNK, 2 * k)
    lower = np.concatenate([mat_im, mat_re], axis=1).reshape(n // CHUNK, 1, CHUNK, 2 * k)
    both = np.concatenate([upper, lower], axis=1).reshape(2 * n, 2 * k)
    return both.astype(np.float32).astype(ml_dtypes.bfloat16)


def constants(size):
    half = size // 2
    kr, ki, fr, fi = tables(size)
    near, far = half + BAND, half - BAND
    prop = [
        packed(kr[:near, :half], ki[:near, :half]),
        packed(kr[far:, half:], ki[far:, half:]),
        packed(kr[:near, :half], -ki[:near, :half]),
        packed(kr[far:, half:], -ki[far:, half:]),
    ]
    four = [
        packed(fr[0::2, :half], fi[0::2, :half]),
        packed(fr[1::2, :half], fi[1::2, :half]),
        packed(fr[:half, 0::2], -fi[:half, 0::2]),
        packed(fr[:half, 1::2], -fi[:half, 1::2]),
    ]
    order = np.concatenate([np.arange(0, size, 2), np.arange(1, size, 2)])
    perm = np.eye(size, dtype=np.float32)[order].astype(ml_dtypes.bfloat16)
    return np.stack(prop), np.stack(four), perm


def nt(left, right):
    return lax.dot_general(left, right, (((1,), (1,)), ((), ())), preferred_element_type=f32)


def banded(prop_ref, base, source):
    size = source.shape[1] // 2
    skip = (size // 2 - BAND) // CHUNK
    stop = (size // 2 + BAND) // CHUNK
    first = nt(prop_ref[base], source[:, :size])
    second = nt(prop_ref[base + 1], source[:, size:])

    def at(j):
        out = []
        for part in range(2):
            value = None
            if j < stop:
                lo = (2 * j + part) * CHUNK
                value = first[lo : lo + CHUNK]
            if j >= skip:
                lo = (2 * (j - skip) + part) * CHUNK
                more = second[lo : lo + CHUNK]
                value = more if value is None else value + more
            out.append(value)
        return out

    return at


def halves(four_ref, base, source):
    size = source.shape[1] // 2
    first = nt(four_ref[base], source[:, :size])
    second = nt(four_ref[base + 1], source[:, size:])

    def at(j):
        lo = 2 * j * CHUNK
        return (
            (first[lo : lo + CHUNK], first[lo + CHUNK : lo + 2 * CHUNK]),
            (second[lo : lo + CHUNK], second[lo + CHUNK : lo + 2 * CHUNK]),
        )

    return at


def put(target, lo, re, im):
    half = re.shape[1] // 2
    target[lo : lo + CHUNK, :] = jnp.concatenate(
        [re[:, :half], im[:, :half], re[:, half:], im[:, half:]], axis=1
    ).astype(bf16)


def put_butterfly(target, lo, re, im):
    half = re.shape[1] // 2
    target[lo : lo + CHUNK, :] = jnp.concatenate(
        [
            re[:, :half] + re[:, half:],
            im[:, :half] + im[:, half:],
            re[:, :half] - re[:, half:],
            im[:, :half] - im[:, half:],
        ],
        axis=1,
    ).astype(bf16)


class Place:
    def __init__(self, row, col):
        self.row = row
        self.block = lax.shift_right_logical(col, 7)
        self.shift = jnp.bitwise_and(col, LANES - 1)


def fill(ext, core, strips, halos):
    strip = strips[0].shape[1]
    for side in range(2):

        @pl.when(core == side)
        def _():
            for part in range(2):
                for block in range(strips[side].shape[2] // LANES):
                    lanes = slice(block * LANES, (block + 1) * LANES)
                    ext[part, block, :strip, :] = strips[side][part, :, lanes].astype(f32)
                    ext[part, block, strip:, :] = halos[side][part, :, lanes].astype(f32)


def window(ext, win, place):
    size = win.shape[1]
    back = jnp.bitwise_and(LANES - place.shift, LANES - 1)
    keep = lax.broadcasted_iota(jnp.int32, (WIN_CHUNK, LANES), 1) < LANES - place.shift
    for lo in range(0, size, WIN_CHUNK):
        span = slice(lo, lo + WIN_CHUNK)
        for part in range(2):
            loaded = [
                pltpu.roll(ext[part, place.block + i, pl.ds(place.row + lo, WIN_CHUNK), :], back, 1)
                for i in range(3)
            ]
            win[part, span, :LANES] = jnp.where(keep, loaded[0], loaded[1])
            win[part, span, LANES:] = jnp.where(keep, loaded[1], loaded[2])


def scatter(acc, place, lo, parts):
    low = lax.broadcasted_iota(jnp.int32, (CHUNK, LANES), 1) < place.shift
    for part, value in enumerate(parts):
        left = pltpu.roll(value[:, :LANES], place.shift, 1)
        right = pltpu.roll(value[:, LANES:], place.shift, 1)
        pieces = (jnp.where(low, 0.0, left), jnp.where(low, left, right), jnp.where(low, right, 0.0))
        for i, piece in enumerate(pieces):
            at = (part, place.block + i, pl.ds(place.row + lo, CHUNK), slice(None))
            acc[at] = acc[at] + piece


def members(step, live):
    for g in range(GROUP):
        slot = step * GROUP + g
        yield jnp.minimum(slot, live - 1), slot < live


def place_of(info_ref, slots, slot):
    return Place(info_ref[2 + slot], info_ref[2 + slots + slot])


def pass_kernel(after_ref, value_ref, out_ref):
    pass


def prepare_kernel(info_ref, meas_ref, perm_ref, probe_ref, prop_ref, four_ref, out_ref):
    perm = perm_ref[...]
    for slot in range(meas_ref.shape[0]):
        rows = jnp.dot(perm, meas_ref[slot], preferred_element_type=f32).astype(bf16)
        out_ref[slot] = nt(rows, perm).astype(bf16)


def positions_kernel(
    info_ref, own_ref, other_ref, halo_own_ref, halo_other_ref, meas_ref, probe_ref, prop_ref, four_ref,
    grads_ref, mine_ref, theirs_ref,
    ext_a, ext_b, win_a, win_b, wave, x_a, x_b, pro, pacc,
):
    size = meas_ref.shape[1]
    half = size // 2
    steps = size // CHUNK
    core, live = info_ref[0], info_ref[1]
    slots = meas_ref.shape[0]
    fill(ext_a, core, (own_ref, other_ref), (halo_own_ref, halo_other_ref))
    fill(ext_b, core, (other_ref, own_ref), (halo_other_ref, halo_own_ref))
    pacc[...] = jnp.zeros(pacc.shape, f32)
    pro[...] = probe_ref[...].astype(f32)

    def visit(step, _):
        group = list(members(step, live))
        for g, (slot, _) in enumerate(group):
            place = place_of(info_ref, slots, slot)
            window(ext_a, win_a.at[g], place)
            window(ext_b, win_b.at[g], place)
            for j in range(steps):
                span = slice(j * CHUNK, (j + 1) * CHUNK)
                pr, pi = pro[0, span], pro[1, span]
                wr, wi = win_a[g, 0, span], win_a[g, 1, span]
                put(x_a.at[g], j * CHUNK, pr * wr - pi * wi, pr * wi + pi * wr)
        for g in range(GROUP):
            at = banded(prop_ref, 0, x_a[g])
            for j in range(steps):
                put(x_b.at[g], j * CHUNK, *at(j))
        for g in range(GROUP):
            at = banded(prop_ref, 0, x_b[g])
            for j in range(steps):
                span = slice(j * CHUNK, (j + 1) * CHUNK)
                re, im = at(j)
                wave[g, 0, span] = re
                wave[g, 1, span] = im
                wr, wi = win_b[g, 0, span], win_b[g, 1, span]
                put_butterfly(x_a.at[g], j * CHUNK, re * wr - im * wi, re * wi + im * wr)
        for g in range(GROUP):
            at = halves(four_ref, 0, x_a[g])
            for j in range(steps // 2):
                even, odd = at(j)
                put_butterfly(x_b.at[g], j * CHUNK, *even)
                put_butterfly(x_b.at[g], half + j * CHUNK, *odd)
        for g, (slot, _) in enumerate(group):
            at = halves(four_ref, 0, x_b[g])
            for j in range(steps // 2):
                for side, (re, im) in enumerate(at(j)):
                    lo = side * half + j * CHUNK
                    misfit = re * re + im * im - meas_ref[slot, lo : lo + CHUNK, :].astype(f32)
                    put(x_a.at[g], lo, misfit * re, misfit * im)
        for g in range(GROUP):
            at = halves(four_ref, 2, x_a[g])
            for j in range(steps // 2):
                (er, ei), (dr, di) = at(j)
                put(x_b.at[g], j * CHUNK, er + dr, ei + di)
                put(x_b.at[g], half + j * CHUNK, er - dr, ei - di)
        for g, (slot, _) in enumerate(group):
            at = halves(four_ref, 2, x_b[g])
            for j in range(steps // 2):
                (er, ei), (dr, di) = at(j)
                for side in range(2):
                    lo = side * half + j * CHUNK
                    span = slice(lo, lo + CHUNK)
                    re, im = (er + dr, ei + di) if side == 0 else (er - dr, ei - di)
                    br, bi = wave[g, 0, span], wave[g, 1, span]
                    wr, wi = win_b[g, 0, span], win_b[g, 1, span]
                    grads_ref[1, slot, 0, span] = (re * br + im * bi).astype(bf16)
                    grads_ref[1, slot, 1, span] = (im * br - re * bi).astype(bf16)
                    put(x_a.at[g], lo, re * wr + im * wi, im * wr - re * wi)
        for g in range(GROUP):
            at = banded(prop_ref, 2, x_a[g])
            for j in range(steps):
                put(x_b.at[g], j * CHUNK, *at(j))
        for g, (slot, valid) in enumerate(group):
            at = banded(prop_ref, 2, x_b[g])
            for j in range(steps):
                span = slice(j * CHUNK, (j + 1) * CHUNK)
                re, im = at(j)
                pr, pi = pro[0, span], pro[1, span]
                grads_ref[0, slot, 0, span] = (re * pr + im * pi).astype(bf16)
                grads_ref[0, slot, 1, span] = (im * pr - re * pi).astype(bf16)
                wr, wi = win_a[g, 0, span], win_a[g, 1, span]
                pacc[0, span] = pacc[0, span] + jnp.where(valid, re * wr + im * wi, 0.0)
                pacc[1, span] = pacc[1, span] + jnp.where(valid, im * wr - re * wi, 0.0)
        return 0

    lax.fori_loop(0, (live + GROUP - 1) // GROUP, visit, 0)
    mine_ref[...] = pacc[core]
    theirs_ref[...] = pacc[1 - core].astype(bf16)


def placing_kernel(own_slice, info_ref, grads_ref, after_ref, strip_ref, tail_ref, token_ref, acc):
    strip, ny = strip_ref.shape[1:]
    slots = grads_ref.shape[1]
    core, live = info_ref[0], info_ref[1]
    which = core if own_slice else 1 - core
    acc[...] = jnp.zeros(acc.shape, f32)

    def visit(slot, _):
        place = place_of(info_ref, slots, slot)
        for lo in range(0, grads_ref.shape[3], CHUNK):
            parts = [grads_ref[which, slot, part, lo : lo + CHUNK, :].astype(f32) for part in range(2)]
            scatter(acc, place, lo, parts)
        return 0

    lax.fori_loop(0, live, visit, 0)
    for part in range(2):
        for block in range(ny // LANES):
            lanes = slice(block * LANES, (block + 1) * LANES)
            strip_ref[part, :, lanes] = acc[part, block, :strip, :].astype(strip_ref.dtype)
            tail_ref[part, :, lanes] = acc[part, block, strip:, :].astype(tail_ref.dtype)
    token_ref[...] = jnp.zeros(token_ref.shape, token_ref.dtype)


def swap(value):
    return lax.ppermute(value, "pos", [(0, 1), (1, 0)])


def shift_tile(value, by):
    peers = lax.axis_size("tile")
    return lax.ppermute(value, "tile", [(i, i + by) for i in range(peers) if 0 <= i + by < peers])


def call(mib, body, results, operands, info, scratch, loose=(), alias=None):
    vmem = pl.BlockSpec(memory_space=pltpu.VMEM)
    smem = pl.BlockSpec(memory_space=pltpu.SMEM)
    spots = [smem] * len(info) + [pl.BlockSpec(memory_space=pl.ANY) if i in loose else vmem for i in range(len(operands))]
    return pl.pallas_call(
        body,
        out_shape=tuple(results),
        in_specs=spots,
        out_specs=(pl.BlockSpec(memory_space=pl.ANY) if alias else vmem,) * len(results),
        scratch_shapes=scratch,
        input_output_aliases=alias or {},
        cost_estimate=pl.CostEstimate(flops=2**20, bytes_accessed=2**12, transcendentals=0),
        compiler_params=pltpu.CompilerParams(vmem_limit_bytes=mib * MIB),
    )(*info, *operands)


def local(object_slices, probe, intensity, scan_rows, scan_cols, counts):
    strip, ny = object_slices.shape[2:]
    size = probe.shape[1]
    slots = intensity.shape[1]
    cores = lax.axis_size("pos")
    core = lax.axis_index("pos")
    peers = lax.axis_size("tile")
    prop, four, perm = (jnp.asarray(t) for t in constants(size))
    sds = jax.ShapeDtypeStruct
    own = object_slices[0]
    live = jnp.minimum(jnp.maximum(counts[0, 0] - core + cores - 1, 0) // cores, slots)
    info = (jnp.concatenate([jnp.stack([core, live]).astype(jnp.int32), scan_rows.reshape(-1), scan_cols.reshape(-1)]),)
    blocks = ny // LANES + 1

    halo_own = shift_tile(own, -1)
    other = swap(own)
    (measured,) = call(
        12,
        prepare_kernel,
        (sds((slots, size, size), bf16),),
        (intensity.reshape(slots, size, size), perm, probe, prop, four),
        info, [],
    )
    (halo_own,) = call(4, pass_kernel, (sds(halo_own.shape, bf16),), (measured, halo_own), (), [], loose=(0, 1), alias={1: 0})
    halo_other = swap(halo_own)

    ext = pltpu.VMEM((2, blocks, 2 * strip, LANES), f32)
    win = pltpu.VMEM((GROUP, 2, size, size), f32)
    half_wave = pltpu.VMEM((GROUP, size, 2 * size), bf16)
    full = pltpu.VMEM((2, size, size), f32)
    grads, mine, theirs = call(
        30,
        positions_kernel,
        (sds((2, slots, 2, size, size), bf16), sds((size, size), f32), sds((size, size), bf16)),
        (own, other, halo_own, halo_other, measured, probe, prop, four),
        info, [ext, ext, win, win, win, half_wave, half_wave, full, full],
    )
    rows = (2, strip, ny)
    flat = sds((size, size), bf16)
    away_strip, away_tail, token = call(
        12,
        functools.partial(placing_kernel, False),
        (sds(rows, bf16), sds(rows, bf16), flat), (grads, grads), info, [ext], loose=(1,),
    )
    part = mine + swap(theirs).astype(f32)
    part = part.astype(bf16)
    own_strip, own_tail, token = call(
        12,
        functools.partial(placing_kernel, True),
        (sds(rows, f32), sds(rows, bf16), flat), (grads, part), info, [ext], loose=(1,),
    )
    above = shift_tile((own_tail.astype(f32) + swap(away_tail).astype(f32)).astype(bf16), 1)
    step = 1
    while step < peers:
        got = lax.ppermute(part, "tile", [(i, i ^ step) for i in range(peers)])
        if 2 * step >= peers:
            (got,) = call(4, pass_kernel, (sds(got.shape, bf16),), (above, got), (), [], loose=(0, 1), alias={1: 0})
        total = part.astype(f32) + got.astype(f32)
        if step == 1:
            total = total + token.astype(f32)
        part = total.astype(bf16)
        step *= 2

    owned = lax.optimization_barrier(own_strip + swap(away_strip).astype(f32))
    owned = owned + above.astype(f32)

    part = total / math.sqrt(peers * slots * cores)
    again = swap(part)
    probe_total = jnp.where(core == 0, jnp.stack([part, again]), jnp.stack([again, part]))
    return owned[None], probe_total


def solution(mesh):
    placed = (
        P("pos", "grp", "tile", None),
        P("grp", None, None),
        P("tile", "grp", "pos", None, None),
        P("tile", "grp", "pos"),
        P("tile", "grp", "pos"),
        P("grp", "tile"),
    )
    return jax.shard_map(
        local,
        mesh=mesh,
        in_specs=placed,
        out_specs=(P("pos", "grp", "tile", None), P("grp", None, None)),
        check_vma=False,
    )
```

```python
import functools
import math

import jax
import jax.numpy as jnp
import ml_dtypes
import numpy as np
from jax import lax
from jax.experimental import pallas as pl
from jax.experimental.pallas import tpu as pltpu
from jax.sharding import PartitionSpec as P

BAND = 32
LANES = 128
CHUNK = 16
WIN_CHUNK = 32
GROUP = 4
MIB = 1024 * 1024
f32 = jnp.float32
bf16 = jnp.bfloat16


def tables(size):
    index = np.arange(size, dtype=np.int32)
    offset = index[:, None] - index[None, :]
    inside = (np.abs(offset) <= BAND).astype(np.float32)
    offset_f = offset.astype(np.float32)
    phase = (np.float32(math.pi) * offset_f * offset_f / np.float32(2.0 * BAND)).astype(np.float32)
    scale = np.float32(1.0 / math.sqrt(2 * BAND + 1))
    prop_re = np.cos(phase) * inside * scale
    prop_im = np.sin(phase) * inside * scale
    product = (index[:, None] * index[None, :]) % size
    angle = (np.float32(-2.0 * math.pi) * product.astype(np.float32) / np.float32(size)).astype(np.float32)
    root = np.float32(math.sqrt(size))
    return prop_re, prop_im, np.cos(angle) / root, np.sin(angle) / root


def packed(mat_re, mat_im):
    n, k = mat_re.shape
    upper = np.concatenate([mat_re, -mat_im], axis=1).reshape(n // CHUNK, 1, CHUNK, 2 * k)
    lower = np.concatenate([mat_im, mat_re], axis=1).reshape(n // CHUNK, 1, CHUNK, 2 * k)
    both = np.concatenate([upper, lower], axis=1).reshape(2 * n, 2 * k)
    return both.astype(np.float32).astype(ml_dtypes.bfloat16)


def constants(size):
    half = size // 2
    kr, ki, fr, fi = tables(size)
    near, far = half + BAND, half - BAND
    prop = [
        packed(kr[:near, :half], ki[:near, :half]),
        packed(kr[far:, half:], ki[far:, half:]),
        packed(kr[:near, :half], -ki[:near, :half]),
        packed(kr[far:, half:], -ki[far:, half:]),
    ]
    four = [
        packed(fr[0::2, :half], fi[0::2, :half]),
        packed(fr[1::2, :half], fi[1::2, :half]),
        packed(fr[:half, 0::2], -fi[:half, 0::2]),
        packed(fr[:half, 1::2], -fi[:half, 1::2]),
    ]
    order = np.concatenate([np.arange(0, size, 2), np.arange(1, size, 2)])
    perm = np.eye(size, dtype=np.float32)[order].astype(ml_dtypes.bfloat16)
    return np.stack(prop), np.stack(four), perm


def nt(left, right):
    return lax.dot_general(left, right, (((1,), (1,)), ((), ())), preferred_element_type=f32)


def banded(prop_ref, base, source):
    size = source.shape[1] // 2
    skip = (size // 2 - BAND) // CHUNK
    stop = (size // 2 + BAND) // CHUNK
    first = nt(prop_ref[base], source[:, :size])
    second = nt(prop_ref[base + 1], source[:, size:])

    def at(j):
        out = []
        for part in range(2):
            value = None
            if j < stop:
                lo = (2 * j + part) * CHUNK
                value = first[lo : lo + CHUNK]
            if j >= skip:
                lo = (2 * (j - skip) + part) * CHUNK
                more = second[lo : lo + CHUNK]
                value = more if value is None else value + more
            out.append(value)
        return out

    return at


def halves(four_ref, base, source):
    size = source.shape[1] // 2
    first = nt(four_ref[base], source[:, :size])
    second = nt(four_ref[base + 1], source[:, size:])

    def at(j):
        lo = 2 * j * CHUNK
        return (
            (first[lo : lo + CHUNK], first[lo + CHUNK : lo + 2 * CHUNK]),
            (second[lo : lo + CHUNK], second[lo + CHUNK : lo + 2 * CHUNK]),
        )

    return at


def put(target, lo, re, im):
    half = re.shape[1] // 2
    target[lo : lo + CHUNK, :] = jnp.concatenate(
        [re[:, :half], im[:, :half], re[:, half:], im[:, half:]], axis=1
    ).astype(bf16)


def put_butterfly(target, lo, re, im):
    half = re.shape[1] // 2
    target[lo : lo + CHUNK, :] = jnp.concatenate(
        [
            re[:, :half] + re[:, half:],
            im[:, :half] + im[:, half:],
            re[:, :half] - re[:, half:],
            im[:, :half] - im[:, half:],
        ],
        axis=1,
    ).astype(bf16)


class Place:
    def __init__(self, row, col):
        self.row = row
        self.block = lax.shift_right_logical(col, 7)
        self.shift = jnp.bitwise_and(col, LANES - 1)


def fill(ext, core, strips, halos):
    strip = strips[0].shape[1]
    for side in range(2):

        @pl.when(core == side)
        def _():
            for part in range(2):
                for block in range(strips[side].shape[2] // LANES):
                    lanes = slice(block * LANES, (block + 1) * LANES)
                    ext[part, block, :strip, :] = strips[side][part, :, lanes].astype(f32)
                    ext[part, block, strip:, :] = halos[side][part, :, lanes].astype(f32)


def window(ext, win, place):
    size = win.shape[1]
    back = jnp.bitwise_and(LANES - place.shift, LANES - 1)
    keep = lax.broadcasted_iota(jnp.int32, (WIN_CHUNK, LANES), 1) < LANES - place.shift
    for lo in range(0, size, WIN_CHUNK):
        span = slice(lo, lo + WIN_CHUNK)
        for part in range(2):
            loaded = [
                pltpu.roll(ext[part, place.block + i, pl.ds(place.row + lo, WIN_CHUNK), :], back, 1)
                for i in range(3)
            ]
            win[part, span, :LANES] = jnp.where(keep, loaded[0], loaded[1])
            win[part, span, LANES:] = jnp.where(keep, loaded[1], loaded[2])


def scatter(acc, place, lo, parts):
    low = lax.broadcasted_iota(jnp.int32, (CHUNK, LANES), 1) < place.shift
    for part, value in enumerate(parts):
        left = pltpu.roll(value[:, :LANES], place.shift, 1)
        right = pltpu.roll(value[:, LANES:], place.shift, 1)
        pieces = (jnp.where(low, 0.0, left), jnp.where(low, left, right), jnp.where(low, right, 0.0))
        for i, piece in enumerate(pieces):
            at = (part, place.block + i, pl.ds(place.row + lo, CHUNK), slice(None))
            acc[at] = acc[at] + piece


def members(step, live):
    for g in range(GROUP):
        slot = step * GROUP + g
        yield jnp.minimum(slot, live - 1), slot < live


def place_of(info_ref, slots, slot):
    return Place(info_ref[2 + slot], info_ref[2 + slots + slot])


def pass_kernel(after_ref, value_ref, out_ref):
    pass


def prepare_kernel(info_ref, meas_ref, perm_ref, probe_ref, prop_ref, four_ref, out_ref):
    perm = perm_ref[...]
    for slot in range(meas_ref.shape[0]):
        rows = jnp.dot(perm, meas_ref[slot], preferred_element_type=f32).astype(bf16)
        out_ref[slot] = nt(rows, perm).astype(bf16)


def positions_kernel(
    info_ref, own_ref, other_ref, halo_own_ref, halo_other_ref, meas_ref, probe_ref, prop_ref, four_ref,
    grads_ref, mine_ref, theirs_ref,
    ext_a, ext_b, win_a, win_b, wave, x_a, x_b, pro, pacc,
):
    size = meas_ref.shape[1]
    half = size // 2
    steps = size // CHUNK
    core, live = info_ref[0], info_ref[1]
    slots = meas_ref.shape[0]
    fill(ext_a, core, (own_ref, other_ref), (halo_own_ref, halo_other_ref))
    fill(ext_b, core, (other_ref, own_ref), (halo_other_ref, halo_own_ref))
    pacc[...] = jnp.zeros(pacc.shape, f32)
    pro[...] = probe_ref[...].astype(f32)

    def visit(step, _):
        group = list(members(step, live))
        places = [place_of(info_ref, slots, slot) for slot, _ in group]
        for g, place in enumerate(places):
            window(ext_a, win_a.at[g], place)
            for j in range(steps):
                span = slice(j * CHUNK, (j + 1) * CHUNK)
                pr, pi = pro[0, span], pro[1, span]
                wr, wi = win_a[g, 0, span], win_a[g, 1, span]
                put(x_a.at[g], j * CHUNK, pr * wr - pi * wi, pr * wi + pi * wr)
            at = banded(prop_ref, 0, x_a[g])
            for j in range(steps):
                put(x_b.at[g], j * CHUNK, *at(j))
        for g in range(GROUP):
            window(ext_b, win_b.at[g], places[g])
            at = banded(prop_ref, 0, x_b[g])
            for j in range(steps):
                span = slice(j * CHUNK, (j + 1) * CHUNK)
                re, im = at(j)
                wave[g, 0, span] = re
                wave[g, 1, span] = im
                wr, wi = win_b[g, 0, span], win_b[g, 1, span]
                put_butterfly(x_a.at[g], j * CHUNK, re * wr - im * wi, re * wi + im * wr)
        for g in range(GROUP):
            at = halves(four_ref, 0, x_a[g])
            for j in range(steps // 2):
                even, odd = at(j)
                put_butterfly(x_b.at[g], j * CHUNK, *even)
                put_butterfly(x_b.at[g], half + j * CHUNK, *odd)
        for g, (slot, _) in enumerate(group):
            at = halves(four_ref, 0, x_b[g])
            for j in range(steps // 2):
                for side, (re, im) in enumerate(at(j)):
                    lo = side * half + j * CHUNK
                    misfit = re * re + im * im - meas_ref[slot, lo : lo + CHUNK, :].astype(f32)
                    put(x_a.at[g], lo, misfit * re, misfit * im)
        for g in range(GROUP):
            at = halves(four_ref, 2, x_a[g])
            for j in range(steps // 2):
                (er, ei), (dr, di) = at(j)
                put(x_b.at[g], j * CHUNK, er + dr, ei + di)
                put(x_b.at[g], half + j * CHUNK, er - dr, ei - di)
        for g, (slot, _) in enumerate(group):
            at = halves(four_ref, 2, x_b[g])
            for j in range(steps // 2):
                (er, ei), (dr, di) = at(j)
                for side in range(2):
                    lo = side * half + j * CHUNK
                    span = slice(lo, lo + CHUNK)
                    re, im = (er + dr, ei + di) if side == 0 else (er - dr, ei - di)
                    br, bi = wave[g, 0, span], wave[g, 1, span]
                    wr, wi = win_b[g, 0, span], win_b[g, 1, span]
                    grads_ref[1, slot, 0, span] = (re * br + im * bi).astype(bf16)
                    grads_ref[1, slot, 1, span] = (im * br - re * bi).astype(bf16)
                    put(x_a.at[g], lo, re * wr + im * wi, im * wr - re * wi)
        for g in range(GROUP):
            at = banded(prop_ref, 2, x_a[g])
            for j in range(steps):
                put(x_b.at[g], j * CHUNK, *at(j))
        for g, (slot, valid) in enumerate(group):
            at = banded(prop_ref, 2, x_b[g])
            for j in range(steps):
                span = slice(j * CHUNK, (j + 1) * CHUNK)
                re, im = at(j)
                pr, pi = pro[0, span], pro[1, span]
                grads_ref[0, slot, 0, span] = (re * pr + im * pi).astype(bf16)
                grads_ref[0, slot, 1, span] = (im * pr - re * pi).astype(bf16)
                wr, wi = win_a[g, 0, span], win_a[g, 1, span]
                pacc[0, span] = pacc[0, span] + jnp.where(valid, re * wr + im * wi, 0.0)
                pacc[1, span] = pacc[1, span] + jnp.where(valid, im * wr - re * wi, 0.0)
        return 0

    lax.fori_loop(0, (live + GROUP - 1) // GROUP, visit, 0)
    mine_ref[...] = pacc[core]
    theirs_ref[...] = pacc[1 - core].astype(bf16)


def placing_kernel(own_slice, info_ref, grads_ref, after_ref, strip_ref, tail_ref, token_ref, acc):
    strip, ny = strip_ref.shape[1:]
    slots = grads_ref.shape[1]
    core, live = info_ref[0], info_ref[1]
    which = core if own_slice else 1 - core
    acc[...] = jnp.zeros(acc.shape, f32)

    def visit(slot, _):
        place = place_of(info_ref, slots, slot)
        for lo in range(0, grads_ref.shape[3], CHUNK):
            parts = [grads_ref[which, slot, part, lo : lo + CHUNK, :].astype(f32) for part in range(2)]
            scatter(acc, place, lo, parts)
        return 0

    lax.fori_loop(0, live, visit, 0)
    for part in range(2):
        for block in range(ny // LANES):
            lanes = slice(block * LANES, (block + 1) * LANES)
            strip_ref[part, :, lanes] = acc[part, block, :strip, :].astype(strip_ref.dtype)
            tail_ref[part, :, lanes] = acc[part, block, strip:, :].astype(tail_ref.dtype)
    token_ref[...] = jnp.zeros(token_ref.shape, token_ref.dtype)


def swap(value):
    return lax.ppermute(value, "pos", [(0, 1), (1, 0)])


def shift_tile(value, by):
    peers = lax.axis_size("tile")
    return lax.ppermute(value, "tile", [(i, i + by) for i in range(peers) if 0 <= i + by < peers])


def call(mib, body, results, operands, info, scratch, loose=(), alias=None):
    moved = 2**22 if mib == 13 else 2**12
    vmem = pl.BlockSpec(memory_space=pltpu.VMEM)
    smem = pl.BlockSpec(memory_space=pltpu.SMEM)
    spots = [smem] * len(info) + [pl.BlockSpec(memory_space=pl.ANY) if i in loose else vmem for i in range(len(operands))]
    return pl.pallas_call(
        body,
        out_shape=tuple(results),
        in_specs=spots,
        out_specs=(pl.BlockSpec(memory_space=pl.ANY) if alias else vmem,) * len(results),
        scratch_shapes=scratch,
        input_output_aliases=alias or {},
        cost_estimate=pl.CostEstimate(flops=2**20, bytes_accessed=moved, transcendentals=0),
        compiler_params=pltpu.CompilerParams(vmem_limit_bytes=mib * MIB),
    )(*info, *operands)


def local(object_slices, probe, intensity, scan_rows, scan_cols, counts):
    strip, ny = object_slices.shape[2:]
    size = probe.shape[1]
    slots = intensity.shape[1]
    cores = lax.axis_size("pos")
    core = lax.axis_index("pos")
    peers = lax.axis_size("tile")
    prop, four, perm = (jnp.asarray(t) for t in constants(size))
    sds = jax.ShapeDtypeStruct
    own = object_slices[0]
    live = jnp.minimum(jnp.maximum(counts[0, 0] - core + cores - 1, 0) // cores, slots)
    info = (jnp.concatenate([jnp.stack([core, live]).astype(jnp.int32), scan_rows.reshape(-1), scan_cols.reshape(-1)]),)
    blocks = ny // LANES + 1

    halo_own = shift_tile(own, -1)
    other = swap(own)
    (measured,) = call(
        12,
        prepare_kernel,
        (sds((slots, size, size), bf16),),
        (intensity.reshape(slots, size, size), perm, probe, prop, four),
        info, [],
    )
    (halo_own,) = call(4, pass_kernel, (sds(halo_own.shape, bf16),), (measured, halo_own), (), [], loose=(0, 1), alias={1: 0})
    halo_other = swap(halo_own)

    ext = pltpu.VMEM((2, blocks, 2 * strip, LANES), f32)
    win = pltpu.VMEM((GROUP, 2, size, size), f32)
    half_wave = pltpu.VMEM((GROUP, size, 2 * size), bf16)
    full = pltpu.VMEM((2, size, size), f32)
    grads, mine, theirs = call(
        30,
        positions_kernel,
        (sds((2, slots, 2, size, size), bf16), sds((size, size), f32), sds((size, size), bf16)),
        (own, other, halo_own, halo_other, measured, probe, prop, four),
        info, [ext, ext, win, win, win, half_wave, half_wave, full, full],
    )
    rows = (2, strip, ny)
    flat = sds((size, size), bf16)
    away_strip, away_tail, token = call(
        13,
        functools.partial(placing_kernel, False),
        (sds(rows, bf16), sds(rows, bf16), flat), (grads, grads), info, [ext], loose=(1,),
    )
    part = mine + swap(theirs).astype(f32)
    part = part.astype(bf16)
    own_strip, own_tail, token = call(
        13,
        functools.partial(placing_kernel, True),
        (sds(rows, f32), sds(rows, bf16), flat), (grads, part), info, [ext], loose=(1,),
    )
    step = 1
    while step < peers:
        got = lax.ppermute(part, "tile", [(i, i ^ step) for i in range(peers)])
        total = part.astype(f32) + got.astype(f32)
        if step == 1:
            total = total + token.astype(f32)
        part = total.astype(bf16)
        step *= 2

    above = shift_tile((own_tail.astype(f32) + swap(away_tail).astype(f32)).astype(bf16), 1)
    owned = lax.optimization_barrier(own_strip + swap(away_strip).astype(f32))
    owned = owned + above.astype(f32)

    part = total / math.sqrt(peers * slots * cores)
    again = swap(part)
    probe_total = jnp.where(core == 0, jnp.stack([part, again]), jnp.stack([again, part]))
    return owned[None], probe_total


def solution(mesh):
    placed = (
        P("pos", "grp", "tile", None),
        P("grp", None, None),
        P("tile", "grp", "pos", None, None),
        P("tile", "grp", "pos"),
        P("tile", "grp", "pos"),
        P("grp", "tile"),
    )
    return jax.shard_map(
        local,
        mesh=mesh,
        in_specs=placed,
        out_specs=(P("pos", "grp", "tile", None), P("grp", None, None)),
        check_vma=False,
    )
```

```python
import functools
import math

import jax
import jax.numpy as jnp
import ml_dtypes
import numpy as np
from jax import lax
from jax.experimental import pallas as pl
from jax.experimental.pallas import tpu as pltpu
from jax.sharding import PartitionSpec as P

BAND = 32
LANES = 128
CHUNK = 16
WIN_CHUNK = 16
GROUP = 4
MIB = 1024 * 1024
f32 = jnp.float32
bf16 = jnp.bfloat16


def tables(size):
    index = np.arange(size, dtype=np.int32)
    offset = index[:, None] - index[None, :]
    inside = (np.abs(offset) <= BAND).astype(np.float32)
    offset_f = offset.astype(np.float32)
    phase = (np.float32(math.pi) * offset_f * offset_f / np.float32(2.0 * BAND)).astype(np.float32)
    scale = np.float32(1.0 / math.sqrt(2 * BAND + 1))
    prop_re = np.cos(phase) * inside * scale
    prop_im = np.sin(phase) * inside * scale
    product = (index[:, None] * index[None, :]) % size
    angle = (np.float32(-2.0 * math.pi) * product.astype(np.float32) / np.float32(size)).astype(np.float32)
    root = np.float32(math.sqrt(size))
    return prop_re, prop_im, np.cos(angle) / root, np.sin(angle) / root


def packed(mat_re, mat_im):
    n, k = mat_re.shape
    upper = np.concatenate([mat_re, -mat_im], axis=1).reshape(n // CHUNK, 1, CHUNK, 2 * k)
    lower = np.concatenate([mat_im, mat_re], axis=1).reshape(n // CHUNK, 1, CHUNK, 2 * k)
    both = np.concatenate([upper, lower], axis=1).reshape(2 * n, 2 * k)
    return both.astype(np.float32).astype(ml_dtypes.bfloat16)


def constants(size):
    half = size // 2
    kr, ki, fr, fi = tables(size)
    near, far = half + BAND, half - BAND
    prop = [
        packed(kr[:near, :half], ki[:near, :half]),
        packed(kr[far:, half:], ki[far:, half:]),
        packed(kr[:near, :half], -ki[:near, :half]),
        packed(kr[far:, half:], -ki[far:, half:]),
    ]
    four = [
        packed(fr[0::2, :half], fi[0::2, :half]),
        packed(fr[1::2, :half], fi[1::2, :half]),
        packed(fr[:half, 0::2], -fi[:half, 0::2]),
        packed(fr[:half, 1::2], -fi[:half, 1::2]),
    ]
    order = np.concatenate([np.arange(0, size, 2), np.arange(1, size, 2)])
    perm = np.eye(size, dtype=np.float32)[order].astype(ml_dtypes.bfloat16)
    return np.stack(prop), np.stack(four), perm


def nt(left, right):
    return lax.dot_general(left, right, (((1,), (1,)), ((), ())), preferred_element_type=f32)


def banded(prop_ref, base, source):
    size = source.shape[1] // 2
    skip = (size // 2 - BAND) // CHUNK
    stop = (size // 2 + BAND) // CHUNK
    first = nt(prop_ref[base], source[:, :size])
    second = nt(prop_ref[base + 1], source[:, size:])

    def at(j):
        out = []
        for part in range(2):
            value = None
            if j < stop:
                lo = (2 * j + part) * CHUNK
                value = first[lo : lo + CHUNK]
            if j >= skip:
                lo = (2 * (j - skip) + part) * CHUNK
                more = second[lo : lo + CHUNK]
                value = more if value is None else value + more
            out.append(value)
        return out

    return at


def halves(four_ref, base, source):
    size = source.shape[1] // 2
    first = nt(four_ref[base], source[:, :size])
    second = nt(four_ref[base + 1], source[:, size:])

    def at(j):
        lo = 2 * j * CHUNK
        return (
            (first[lo : lo + CHUNK], first[lo + CHUNK : lo + 2 * CHUNK]),
            (second[lo : lo + CHUNK], second[lo + CHUNK : lo + 2 * CHUNK]),
        )

    return at


def put(target, lo, re, im):
    half = re.shape[1] // 2
    target[lo : lo + CHUNK, :] = jnp.concatenate(
        [re[:, :half], im[:, :half], re[:, half:], im[:, half:]], axis=1
    ).astype(bf16)


def put_butterfly(target, lo, re, im):
    half = re.shape[1] // 2
    target[lo : lo + CHUNK, :] = jnp.concatenate(
        [
            re[:, :half] + re[:, half:],
            im[:, :half] + im[:, half:],
            re[:, :half] - re[:, half:],
            im[:, :half] - im[:, half:],
        ],
        axis=1,
    ).astype(bf16)


class Place:
    def __init__(self, row, col):
        self.row = row
        self.block = lax.shift_right_logical(col, 7)
        self.shift = jnp.bitwise_and(col, LANES - 1)


def fill(ext, core, strips, halos):
    strip = strips[0].shape[1]
    for side in range(2):

        @pl.when(core == side)
        def _():
            for part in range(2):
                for block in range(strips[side].shape[2] // LANES):
                    lanes = slice(block * LANES, (block + 1) * LANES)
                    ext[part, block, :strip, :] = strips[side][part, :, lanes].astype(f32)
                    ext[part, block, strip:, :] = halos[side][part, :, lanes].astype(f32)


def window(ext, win, place):
    size = win.shape[1]
    back = jnp.bitwise_and(LANES - place.shift, LANES - 1)
    keep = lax.broadcasted_iota(jnp.int32, (WIN_CHUNK, LANES), 1) < LANES - place.shift
    for lo in range(0, size, WIN_CHUNK):
        span = slice(lo, lo + WIN_CHUNK)
        for part in range(2):
            loaded = [
                pltpu.roll(ext[part, place.block + i, pl.ds(place.row + lo, WIN_CHUNK), :], back, 1)
                for i in range(3)
            ]
            win[part, span, :LANES] = jnp.where(keep, loaded[0], loaded[1])
            win[part, span, LANES:] = jnp.where(keep, loaded[1], loaded[2])


def scatter(acc, place, lo, parts):
    low = lax.broadcasted_iota(jnp.int32, (CHUNK, LANES), 1) < place.shift
    for part, value in enumerate(parts):
        left = pltpu.roll(value[:, :LANES], place.shift, 1)
        right = pltpu.roll(value[:, LANES:], place.shift, 1)
        pieces = (jnp.where(low, 0.0, left), jnp.where(low, left, right), jnp.where(low, right, 0.0))
        for i, piece in enumerate(pieces):
            at = (part, place.block + i, pl.ds(place.row + lo, CHUNK), slice(None))
            acc[at] = acc[at] + piece


def members(step, live):
    for g in range(GROUP):
        slot = step * GROUP + g
        yield jnp.minimum(slot, live - 1), slot < live


def place_of(info_ref, slots, slot):
    return Place(info_ref[2 + slot], info_ref[2 + slots + slot])


def pass_kernel(after_ref, value_ref, out_ref):
    pass


def prepare_kernel(info_ref, meas_ref, perm_ref, probe_ref, prop_ref, four_ref, out_ref):
    perm = perm_ref[...]
    for slot in range(meas_ref.shape[0]):
        rows = jnp.dot(perm, meas_ref[slot], preferred_element_type=f32).astype(bf16)
        out_ref[slot] = nt(rows, perm).astype(bf16)


def positions_kernel(
    info_ref, own_ref, other_ref, halo_own_ref, halo_other_ref, meas_ref, probe_ref, prop_ref, four_ref,
    grads_ref, mine_ref, theirs_ref,
    ext_a, ext_b, win_a, win_b, wave, x_a, x_b, pro, pacc,
):
    size = meas_ref.shape[1]
    half = size // 2
    steps = size // CHUNK
    core, live = info_ref[0], info_ref[1]
    slots = meas_ref.shape[0]
    fill(ext_a, core, (own_ref, other_ref), (halo_own_ref, halo_other_ref))
    fill(ext_b, core, (other_ref, own_ref), (halo_other_ref, halo_own_ref))
    pacc[...] = jnp.zeros(pacc.shape, f32)
    pro[...] = probe_ref[...].astype(f32)

    def visit(step, _):
        group = list(members(step, live))
        places = [place_of(info_ref, slots, slot) for slot, _ in group]
        for g, place in enumerate(places):
            window(ext_a, win_a.at[g], place)
            for j in range(steps):
                span = slice(j * CHUNK, (j + 1) * CHUNK)
                pr, pi = pro[0, span], pro[1, span]
                wr, wi = win_a[g, 0, span], win_a[g, 1, span]
                put(x_a.at[g], j * CHUNK, pr * wr - pi * wi, pr * wi + pi * wr)
            at = banded(prop_ref, 0, x_a[g])
            for j in range(steps):
                put(x_b.at[g], j * CHUNK, *at(j))
        for g in range(GROUP):
            window(ext_b, win_b.at[g], places[g])
            at = banded(prop_ref, 0, x_b[g])
            for j in range(steps):
                span = slice(j * CHUNK, (j + 1) * CHUNK)
                re, im = at(j)
                wave[g, 0, span] = re
                wave[g, 1, span] = im
                wr, wi = win_b[g, 0, span], win_b[g, 1, span]
                put_butterfly(x_a.at[g], j * CHUNK, re * wr - im * wi, re * wi + im * wr)
        for g in range(GROUP):
            at = halves(four_ref, 0, x_a[g])
            for j in range(steps // 2):
                even, odd = at(j)
                put_butterfly(x_b.at[g], j * CHUNK, *even)
                put_butterfly(x_b.at[g], half + j * CHUNK, *odd)
        for g, (slot, _) in enumerate(group):
            at = halves(four_ref, 0, x_b[g])
            for j in range(steps // 2):
                for side, (re, im) in enumerate(at(j)):
                    lo = side * half + j * CHUNK
                    misfit = re * re + im * im - meas_ref[slot, lo : lo + CHUNK, :].astype(f32)
                    put(x_a.at[g], lo, misfit * re, misfit * im)
        for g in range(GROUP):
            at = halves(four_ref, 2, x_a[g])
            for j in range(steps // 2):
                (er, ei), (dr, di) = at(j)
                put(x_b.at[g], j * CHUNK, er + dr, ei + di)
                put(x_b.at[g], half + j * CHUNK, er - dr, ei - di)
        for g, (slot, _) in enumerate(group):
            at = halves(four_ref, 2, x_b[g])
            for j in range(steps // 2):
                (er, ei), (dr, di) = at(j)
                for side in range(2):
                    lo = side * half + j * CHUNK
                    span = slice(lo, lo + CHUNK)
                    re, im = (er + dr, ei + di) if side == 0 else (er - dr, ei - di)
                    br, bi = wave[g, 0, span], wave[g, 1, span]
                    wr, wi = win_b[g, 0, span], win_b[g, 1, span]
                    grads_ref[1, slot, 0, span] = (re * br + im * bi).astype(bf16)
                    grads_ref[1, slot, 1, span] = (im * br - re * bi).astype(bf16)
                    put(x_a.at[g], lo, re * wr + im * wi, im * wr - re * wi)
        for g in range(GROUP):
            at = banded(prop_ref, 2, x_a[g])
            for j in range(steps):
                put(x_b.at[g], j * CHUNK, *at(j))
        for g, (slot, valid) in enumerate(group):
            at = banded(prop_ref, 2, x_b[g])
            for j in range(steps):
                span = slice(j * CHUNK, (j + 1) * CHUNK)
                re, im = at(j)
                pr, pi = pro[0, span], pro[1, span]
                grads_ref[0, slot, 0, span] = (re * pr + im * pi).astype(bf16)
                grads_ref[0, slot, 1, span] = (im * pr - re * pi).astype(bf16)
                wr, wi = win_a[g, 0, span], win_a[g, 1, span]
                pacc[0, span] = pacc[0, span] + jnp.where(valid, re * wr + im * wi, 0.0)
                pacc[1, span] = pacc[1, span] + jnp.where(valid, im * wr - re * wi, 0.0)
        return 0

    lax.fori_loop(0, (live + GROUP - 1) // GROUP, visit, 0)
    mine_ref[...] = pacc[core]
    theirs_ref[...] = pacc[1 - core].astype(bf16)


def placing_kernel(own_slice, info_ref, grads_ref, after_ref, strip_ref, tail_ref, token_ref, acc):
    strip, ny = strip_ref.shape[1:]
    slots = grads_ref.shape[1]
    core, live = info_ref[0], info_ref[1]
    which = core if own_slice else 1 - core
    acc[...] = jnp.zeros(acc.shape, f32)

    def visit(slot, _):
        place = place_of(info_ref, slots, slot)
        for lo in range(0, grads_ref.shape[3], CHUNK):
            parts = [grads_ref[which, slot, part, lo : lo + CHUNK, :].astype(f32) for part in range(2)]
            scatter(acc, place, lo, parts)
        return 0

    lax.fori_loop(0, live, visit, 0)
    for part in range(2):
        for block in range(ny // LANES):
            lanes = slice(block * LANES, (block + 1) * LANES)
            strip_ref[part, :, lanes] = acc[part, block, :strip, :].astype(strip_ref.dtype)
            tail_ref[part, :, lanes] = acc[part, block, strip:, :].astype(tail_ref.dtype)
    token_ref[...] = jnp.zeros(token_ref.shape, token_ref.dtype)


def swap(value):
    return lax.ppermute(value, "pos", [(0, 1), (1, 0)])


def shift_tile(value, by):
    peers = lax.axis_size("tile")
    return lax.ppermute(value, "tile", [(i, i + by) for i in range(peers) if 0 <= i + by < peers])


def call(mib, body, results, operands, info, scratch, loose=(), alias=None):
    moved = 2**22 if mib == 13 else 2**12
    vmem = pl.BlockSpec(memory_space=pltpu.VMEM)
    smem = pl.BlockSpec(memory_space=pltpu.SMEM)
    spots = [smem] * len(info) + [pl.BlockSpec(memory_space=pl.ANY) if i in loose else vmem for i in range(len(operands))]
    return pl.pallas_call(
        body,
        out_shape=tuple(results),
        in_specs=spots,
        out_specs=(pl.BlockSpec(memory_space=pl.ANY) if alias else vmem,) * len(results),
        scratch_shapes=scratch,
        input_output_aliases=alias or {},
        cost_estimate=pl.CostEstimate(flops=2**20, bytes_accessed=moved, transcendentals=0),
        compiler_params=pltpu.CompilerParams(vmem_limit_bytes=mib * MIB),
    )(*info, *operands)


def local(object_slices, probe, intensity, scan_rows, scan_cols, counts):
    strip, ny = object_slices.shape[2:]
    size = probe.shape[1]
    slots = intensity.shape[1]
    cores = lax.axis_size("pos")
    core = lax.axis_index("pos")
    peers = lax.axis_size("tile")
    prop, four, perm = (jnp.asarray(t) for t in constants(size))
    sds = jax.ShapeDtypeStruct
    own = object_slices[0]
    live = jnp.minimum(jnp.maximum(counts[0, 0] - core + cores - 1, 0) // cores, slots)
    info = (jnp.concatenate([jnp.stack([core, live]).astype(jnp.int32), scan_rows.reshape(-1), scan_cols.reshape(-1)]),)
    blocks = ny // LANES + 1

    halo_own = shift_tile(own, -1)
    other = swap(own)
    (measured,) = call(
        12,
        prepare_kernel,
        (sds((slots, size, size), bf16),),
        (intensity.reshape(slots, size, size), perm, probe, prop, four),
        info, [],
    )
    (halo_own,) = call(4, pass_kernel, (sds(halo_own.shape, bf16),), (measured, halo_own), (), [], loose=(0, 1), alias={1: 0})
    halo_other = swap(halo_own)

    ext = pltpu.VMEM((2, blocks, 2 * strip, LANES), f32)
    win = pltpu.VMEM((GROUP, 2, size, size), f32)
    half_wave = pltpu.VMEM((GROUP, size, 2 * size), bf16)
    full = pltpu.VMEM((2, size, size), f32)
    grads, mine, theirs = call(
        30,
        positions_kernel,
        (sds((2, slots, 2, size, size), bf16), sds((size, size), f32), sds((size, size), bf16)),
        (own, other, halo_own, halo_other, measured, probe, prop, four),
        info, [ext, ext, win, win, win, half_wave, half_wave, full, full],
    )
    rows = (2, strip, ny)
    flat = sds((size, size), bf16)
    away_strip, away_tail, token = call(
        13,
        functools.partial(placing_kernel, False),
        (sds(rows, bf16), sds(rows, bf16), flat), (grads, grads), info, [ext], loose=(1,),
    )
    part = mine + swap(theirs).astype(f32)
    part = part.astype(bf16)
    own_strip, own_tail, token = call(
        13,
        functools.partial(placing_kernel, True),
        (sds(rows, f32), sds(rows, bf16), flat), (grads, part), info, [ext], loose=(1,),
    )
    step = 1
    while step < peers:
        got = lax.ppermute(part, "tile", [(i, i ^ step) for i in range(peers)])
        total = part.astype(f32) + got.astype(f32)
        if step == 1:
            total = total + token.astype(f32)
        part = total.astype(bf16)
        step *= 2

    above = shift_tile((own_tail.astype(f32) + swap(away_tail).astype(f32)).astype(bf16), 1)
    owned = lax.optimization_barrier(own_strip + swap(away_strip).astype(f32))
    owned = owned + above.astype(f32)

    part = total / math.sqrt(peers * slots * cores)
    again = swap(part)
    probe_total = jnp.where(core == 0, jnp.stack([part, again]), jnp.stack([again, part]))
    return owned[None], probe_total


def solution(mesh):
    placed = (
        P("pos", "grp", "tile", None),
        P("grp", None, None),
        P("tile", "grp", "pos", None, None),
        P("tile", "grp", "pos"),
        P("tile", "grp", "pos"),
        P("grp", "tile"),
    )
    return jax.shard_map(
        local,
        mesh=mesh,
        in_specs=placed,
        out_specs=(P("pos", "grp", "tile", None), P("grp", None, None)),
        check_vma=False,
    )
```
